32 devices in a mesh: parts: 2 (over x), wide: 8 (over z, y), narrow: 2 (over core).
Axes of the slice: x: 2, y: 2, z: 4, core: 2. Of those that a mesh axis runs over, the one named last changes fastest.
Arguments:
- token_ids: int32 [2048], P('parts'), parts along dimension 0, may hold values from 0 to 128255, as said below
- slab_offset: int32 [2], P('parts'), parts along dimension 0, may hold values from 0 to 26496, as said below
- activations: bfloat16 [2048, 8192], P(('parts', 'wide')), parts along dimension 0, may hold values from -6 to 6
- gate_weight: bfloat16 [8192, 26624], P(None, ('wide', 'narrow')), may hold values from -0.0625 to 0.0625
- up_weight: bfloat16 [8192, 26624], P(None, ('wide', 'narrow')), may hold values from -0.0625 to 0.0625
- prior_slab: float32 [256, 26624], P(('parts', 'narrow'), 'wide'), parts along dimension 0, may hold values from -48 to 48
Outputs:
- new_slab: float32 [256, 26624], P(('parts', 'narrow'), 'wide'), parts along dimension 0
The draws below stay inside these ranges and needn't reach their ends.
There are 2 independent parts, one for each index of `parts`. The reference program is written for one: setup_inputs(seed, part) draws one part's arguments, and reference() takes and returns one part's arrays. A program takes and returns all parts, laid end to end along the dimension named above; an argument that names none is the same for every part. Nothing has to cross between parts.
Inputs may be any that keep to these rules, and one draw needn't show every extreme that they name: `token_ids`: ids at or above 128000 are special tokens. `slab_offset`: A multiple of 64.
All inputs are finite; a program needn't handle non-finite values.
Results may differ from the reference program's by a relative error of at most 0.0039.
Values may be sent and summed in bfloat16 or wider, within the bound.
A program may use at most 192 MiB of HBM per device.

```python
import jax
import jax.numpy as jnp
from jax import lax

D = 8192
FFW = 26624
TOK = 1024
HALF = 64
SLAB = 128


def draw_token_ids(key, part):
    key = jax.random.fold_in(key, 11)
    first_key, second_key, third_key = jax.random.split(key, 3)
    category = jax.random.randint(first_key, (TOK,), 0, 8)
    drawn = jax.random.randint(second_key, (TOK,), 0, 128000)
    special = jax.random.randint(third_key, (TOK,), 128000, 128256)
    return jnp.where(category == 0, special, drawn).astype(jnp.int32)


def draw_slab_offset(key, part):
    key = jax.random.fold_in(key, 12)
    positions = (FFW - SLAB) // HALF + 1
    return (HALF * jax.random.randint(key, (1,), 0, positions)).astype(jnp.int32)


def shard_levels(rng, shape, cuts, low, top_value):
    def one(dim, blocks):
        draws = jax.random.uniform(jax.random.fold_in(jax.random.fold_in(rng, 6), dim), (blocks,), jnp.float32, low / len(cuts), top_value / len(cuts))
        return jnp.repeat(jnp.exp(draws), shape[dim] // blocks).reshape((-1,) + (1,) * (len(shape) - dim - 1))

    level = one(*cuts[0])
    for cut in cuts[1:]:
        level = level * one(*cut)
    return level


def bell_draw(rng, shape, scale, bound, pieces=(), kind=jnp.bfloat16):
    array = scale * jax.random.normal(rng, shape, jnp.float32)
    if pieces:
        array = array * shard_levels(rng, shape, pieces, -0.22, 0.18)
    return jnp.clip(array, -bound, bound).astype(kind)


def setup_inputs(seed: int = 0, part: int = 0) -> dict:
    key_list = jax.random.split(jax.random.key(seed), 7)
    part_splits = jax.random.split(jax.random.fold_in(key_list[6], part), 7)
    token_ids = draw_token_ids(jax.random.fold_in(jax.random.fold_in(key_list[6], part), 71), part)
    slab_offset = draw_slab_offset(jax.random.fold_in(jax.random.fold_in(key_list[6], part), 71), part)
    activations = bell_draw(part_splits[2], (TOK, D), 1.0, 6.0, ((0, 8),))
    gate_weight = bell_draw(key_list[3], (D, FFW), D ** -0.5, 0.0625, ((1, 16),))
    up_weight = bell_draw(key_list[4], (D, FFW), D ** -0.5, 0.0625, ((1, 16),))
    prior_slab = bell_draw(part_splits[5], (SLAB, FFW), 8.0, 48.0, ((0, 2), (1, 8)), jnp.float32)
    return dict(token_ids=token_ids, slab_offset=slab_offset, activations=activations, gate_weight=gate_weight, up_weight=up_weight, prior_slab=prior_slab)


special_first = 128000


def reference(token_ids, slab_offset, activations, gate_weight, up_weight, prior_slab):
    gate_sum = jnp.dot(activations, gate_weight, preferred_element_type=jnp.float32)
    up_sum = jnp.dot(activations, up_weight, preferred_element_type=jnp.float32)
    key_rows = (jax.nn.silu(gate_sum) * up_sum).astype(jnp.bfloat16)
    selected = lax.dynamic_slice_in_dim(key_rows, slab_offset[0].astype(jnp.int32), SLAB, 1)
    usable = (token_ids < special_first).astype(jnp.bfloat16)[:, None]
    masked = selected * usable
    product = lax.dot_general(masked, key_rows, (((0,), (0,)), ((), ())), preferred_element_type=jnp.float32)
    return prior_slab + product
```

```python
import functools

import jax
import jax.numpy as jnp
from jax import lax
from jax.experimental import pallas as pl
from jax.experimental.pallas import tpu as pltpu
from jax.sharding import PartitionSpec as P

special_first = 128000
LINE = 4
PAIR = 2
MESH = pl.DeviceIdType.MESH


def make_keys(features, gate_weight, up_weight):
    gate_sum = jnp.dot(features, gate_weight, preferred_element_type=jnp.float32)
    up_sum = jnp.dot(features, up_weight, preferred_element_type=jnp.float32)
    return (jax.nn.silu(gate_sum) * up_sum).astype(jnp.bfloat16)


def plain_shards(token_ids, slab_offset, activations, gate_weight, up_weight, prior_slab):
    key_rows = make_keys(
        lax.all_gather(activations, "wide", axis=0, tiled=True), gate_weight, up_weight
    )
    columns = lax.all_gather(key_rows, "narrow", axis=1, tiled=True)
    column_count = columns.shape[1]
    row_count = prior_slab.shape[0]
    row_first = slab_offset[0] + lax.axis_index("narrow") * row_count
    holder = row_first // column_count
    inside = row_first % column_count
    candidate = lax.dynamic_slice_in_dim(columns, inside, row_count, 1)
    contribution = jnp.where(
        lax.axis_index("wide") == holder, candidate.astype(jnp.float32), jnp.float32(0.0)
    )
    selected = lax.psum(contribution.astype(jnp.bfloat16), "wide")
    usable = (token_ids < special_first).astype(jnp.bfloat16)[:, None]
    masked = selected * usable
    product = lax.dot_general(
        masked, columns, (((0,), (0,)), ((), ())), preferred_element_type=jnp.float32
    )
    return prior_slab + product


def keys_kernel(
    act, wg, wu, keys, gath, w_v, x_v, k_v,
    w_sem, x_sem, k_sem, up_send, up_recv, down_send, down_recv, side_send, side_recv,
    core_send, core_recv,
):
    wide = lax.axis_index("wide")
    core = lax.axis_index("narrow")
    z, y = wide // PAIR, wide % PAIR
    rows = act.shape[0]
    half = rows // 2
    tiles = w_v.shape[0]
    up = lax.rem(z + 1, LINE) * PAIR + y
    down = lax.rem(z + LINE - 1, LINE) * PAIR + y
    side = z * PAIR + 1 - y

    barrier = pltpu.get_barrier_semaphore()
    for w in (up, down, side):
        pl.semaphore_signal(
            barrier, inc=1, device_id={"wide": w, "narrow": core}, device_id_type=MESH
        )
    pl.semaphore_signal(
        barrier, inc=1, device_id={"wide": wide, "narrow": 1 - core}, device_id_type=MESH
    )

    def x_copy(src, slot, k):
        return pltpu.make_async_copy(
            src, x_v.at[slot, pl.ds(k * rows, rows), :], x_sem.at[slot, k]
        )

    x_copy(act, 0, 0).start()

    def w_copy(t, k):
        src = (wg, wu)[k]
        return pltpu.make_async_copy(
            src.at[:, pl.ds(pl.multiple_of(t * 128, 128), 128)],
            w_v.at[t, :, pl.ds(k * 128, 128)],
            w_sem.at[k, t],
        )

    @pl.loop(0, tiles)
    def _(t):
        w_copy(t, 0).start()
        w_copy(t, 1).start()

    pl.semaphore_wait(barrier, 4)

    def half_rows(b, c):
        return pl.ds(pl.multiple_of(b * rows + c * half, 16), half)

    order = (z, z + 1 - 2 * lax.rem(z, 2), 2 - z // 2, 3 - 3 * (z // 2))

    def send(kind, r):
        block = {"up": z - r, "down": z + r, "side": order[r]}[kind]
        target = {"up": up, "down": down, "side": side}[kind]
        ss, rs = {
            "up": (up_send, up_recv), "down": (down_send, down_recv), "side": (side_send, side_recv)
        }[kind]
        b = block * PAIR + y
        if r == 0:
            src = act.at[pl.ds(pl.multiple_of(core * half, 16), half), :]
        else:
            src = gath.at[half_rows(b, core), :]
        return pltpu.make_async_remote_copy(
            src_ref=src, dst_ref=gath.at[half_rows(b, core), :],
            send_sem=ss.at[r], recv_sem=rs.at[r],
            device_id={"wide": target, "narrow": core}, device_id_type=MESH,
        )

    def share(b):
        part = gath.at[half_rows(b, core), :]
        return pltpu.make_async_remote_copy(
            src_ref=part, dst_ref=part, send_sem=core_send.at[b], recv_sem=core_recv.at[b],
            device_id={"wide": wide, "narrow": 1 - core}, device_id_type=MESH,
        )

    def sends(kind, r):
        if kind == "up":
            return jnp.logical_and(z - r >= 0, z < LINE - 1)
        return jnp.logical_and(z + r < LINE, z > 0)

    def receives(kind, r):
        return z - 1 - r >= 0 if kind == "up" else z + 1 + r < LINE

    def push(r):
        send("side", r).start()
        if r < LINE - 1:
            for kind in ("up", "down"):
                @pl.when(sends(kind, r))
                def _():
                    send(kind, r).start()

    def arrive(r):
        if r < LINE - 1:
            for kind in ("up", "down"):
                @pl.when(receives(kind, r))
                def _():
                    send(kind, r).wait_recv()
        send("side", r).wait_recv()

    def spread(r):
        if r < LINE - 1:
            for kind in ("up", "down"):
                @pl.when(receives(kind, r))
                def _():
                    block = z - 1 - r if kind == "up" else z + 1 + r
                    share(block * PAIR + y).start()
        share(order[r] * PAIR + 1 - y).start()

    def tile(t, count, slot):
        acc = jnp.dot(x_v[slot, :count, :], w_v[t], preferred_element_type=jnp.float32)
        g, u = acc[:, :128], acc[:, 128:]
        k_v[:count, pl.ds(pl.multiple_of(t * 128, 128), 128)] = (
            g / (1.0 + jnp.exp(-g)) * u
        ).astype(jnp.bfloat16)

    def k_copy(b, k):
        return pltpu.make_async_copy(
            k_v.at[pl.ds(k * rows, rows), :],
            keys.at[pl.ds(pl.multiple_of(b * rows, 16), rows), :],
            k_sem.at[k],
        )

    push(0)
    x_copy(act, 0, 0).wait()

    @pl.loop(0, tiles)
    def _(t):
        w_copy(t, 0).wait()
        w_copy(t, 1).wait()
        tile(t, rows, 0)

    done = [k_copy(z * PAIR + y, 0)]
    done[0].start()
    for r in range(LINE):
        arrive(r)
        if r < LINE - 1:
            push(r + 1)
        spread(r)
        slot = (r + 1) % 2
        blocks = [order[r] * PAIR + 1 - y]
        if r < LINE - 1:
            blocks.append(order[r + 1] * PAIR + y)
        loads = []
        for k, b in enumerate(blocks):
            share(b).wait_recv()
            load = x_copy(gath.at[pl.ds(pl.multiple_of(b * rows, 16), rows), :], slot, k)
            load.start()
            loads.append(load)
        for load in loads:
            load.wait()
        for copy in done:
            copy.wait()

        @pl.loop(0, tiles)
        def _(t):
            tile(t, rows * len(blocks), slot)

        done = [k_copy(b, k) for k, b in enumerate(blocks)]
        for copy in done:
            copy.start()
    for copy in done:
        copy.wait()
    for r in range(LINE):
        send("side", r).wait_send()
        share(order[r] * PAIR + 1 - y).wait_send()
        if r:
            share(order[r] * PAIR + y).wait_send()
        if r < LINE - 1:
            for kind in ("up", "down"):
                @pl.when(sends(kind, r))
                def _():
                    send(kind, r).wait_send()


def make_key_rows(activations, gate_weight, up_weight):
    rows, features = activations.shape
    units = gate_weight.shape[1]
    tiles = units // 128
    tokens = rows * LINE * PAIR
    dma = pltpu.SemaphoreType.DMA
    return pl.pallas_call(
        keys_kernel,
        out_shape=(
            jax.ShapeDtypeStruct((tokens, units), jnp.bfloat16),
            jax.ShapeDtypeStruct((tokens, features), jnp.bfloat16),
        ),
        in_specs=[pl.BlockSpec(memory_space=pl.ANY)] * 3,
        out_specs=(pl.BlockSpec(memory_space=pl.ANY),) * 2,
        scratch_shapes=[
            pltpu.VMEM((tiles, features, 256), jnp.bfloat16),
            pltpu.VMEM((2, 2 * rows, features), jnp.bfloat16),
            pltpu.VMEM((2 * rows, units), jnp.bfloat16),
            dma((2, tiles)), dma((2, 2)), dma((2,)),
            dma((LINE - 1,)), dma((LINE - 1,)), dma((LINE - 1,)), dma((LINE - 1,)),
            dma((LINE,)), dma((LINE,)), dma((LINE * PAIR,)), dma((LINE * PAIR,)),
        ],
        compiler_params=pltpu.CompilerParams(
            collective_id=0, has_side_effects=True, vmem_limit_bytes=63 * 1024 * 1024
        ),
        name="gather_keys",
    )(activations, gate_weight, up_weight)[0]


def slab_kernel(
    group, contribution, usable, keys, prior, out, land, sel, product, other,
    first_send, first_recv, second_send, second_recv, swap_send, swap_recv,
):
    wide = lax.axis_index("wide")
    core = lax.axis_index("narrow")
    me = wide * 2 + core
    span = land.shape[1]
    row_count = prior.shape[0]
    units = keys.shape[1]

    def rows_of(g):
        return pl.ds(pl.multiple_of(g * span, 16), span)

    def device(g):
        return {"wide": g // 2, "narrow": lax.rem(g, 2)}

    barrier = pltpu.get_barrier_semaphore()

    @pl.loop(1, group)
    def _(j):
        pl.semaphore_signal(
            barrier, inc=1, device_id=device(lax.rem(me + j, group)), device_id_type=MESH
        )

    pl.semaphore_wait(barrier, group - 1)

    def first(j):
        target = lax.rem(me + j, group)
        return pltpu.make_async_remote_copy(
            src_ref=contribution.at[rows_of(target), :], dst_ref=land.at[j - 1],
            send_sem=first_send.at[j - 1], recv_sem=first_recv.at[j - 1],
            device_id=device(target), device_id_type=MESH,
        )

    def second(j, owner):
        return pltpu.make_async_remote_copy(
            src_ref=sel.at[rows_of(owner), :], dst_ref=sel.at[rows_of(owner), :],
            send_sem=second_send.at[j - 1], recv_sem=second_recv.at[j - 1],
            device_id=device(lax.rem(me + j, group)), device_id_type=MESH,
        )

    @pl.loop(1, group)
    def _(j):
        first(j).start()

    @pl.loop(1, group)
    def _(j):
        first(j).wait_recv()

    total = contribution[rows_of(me), :].astype(jnp.float32)
    for j in range(1, group):
        total = total + land[j - 1].astype(jnp.float32)
    sel[rows_of(me), :] = (total * usable[rows_of(me), :]).astype(jnp.bfloat16)

    @pl.loop(1, group)
    def _(j):
        second(j, me).start()

    @pl.loop(1, group)
    def _(j):
        second(j, lax.rem(me + group - j, group)).wait_recv()

    product[...] = lax.dot_general(
        sel[...], keys[...], (((0,), (0,)), ((), ())), preferred_element_type=jnp.float32
    ).reshape(2, row_count, units)

    swap = pltpu.make_async_remote_copy(
        src_ref=product.at[1 - core], dst_ref=other,
        send_sem=swap_send, recv_sem=swap_recv,
        device_id={"wide": wide, "narrow": 1 - core}, device_id_type=MESH,
    )
    swap.start()
    mine = pl.ds(pl.multiple_of(core * units, 128), units)
    theirs = pl.ds(pl.multiple_of((1 - core) * units, 128), units)
    out[:, mine] = prior[:, mine] + product[core]
    swap.wait_recv()
    out[:, theirs] = prior[:, theirs] + other[...]
    swap.wait_send()

    @pl.loop(1, group)
    def _(j):
        first(j).wait_send()
        second(j, me).wait_send()


def add_slab(group, contribution, usable, keys, prior):
    tokens, units = keys.shape
    row_count, slab_columns = prior.shape
    span = tokens // group
    dma = pltpu.SemaphoreType.DMA
    vmem = pl.BlockSpec(memory_space=pltpu.VMEM)
    return pl.pallas_call(
        functools.partial(slab_kernel, group),
        out_shape=jax.ShapeDtypeStruct(prior.shape, jnp.float32),
        in_specs=[vmem] * 4,
        out_specs=vmem,
        scratch_shapes=[
            pltpu.VMEM((group - 1, span, 2 * row_count), jnp.bfloat16),
            pltpu.VMEM((tokens, 2 * row_count), jnp.bfloat16),
            pltpu.VMEM((2, row_count, units), jnp.float32),
            pltpu.VMEM((row_count, units), jnp.float32),
            dma((group - 1,)), dma((group - 1,)), dma((group - 1,)), dma((group - 1,)),
            dma, dma,
        ],
        compiler_params=pltpu.CompilerParams(
            collective_id=1, has_side_effects=True, vmem_limit_bytes=40 * 1024 * 1024
        ),
        name="slab_product",
    )(contribution, usable, keys, prior)


def fused_shards(token_ids, slab_offset, activations, gate_weight, up_weight, prior_slab):
    keys = make_key_rows(activations, gate_weight, up_weight)
    units = keys.shape[1]
    row_count = prior_slab.shape[0]
    me = lax.axis_index("wide") * 2 + lax.axis_index("narrow")
    pieces = []
    for k in range(2):
        row_first = slab_offset[0] + k * row_count
        candidate = lax.dynamic_slice_in_dim(keys, row_first % units, row_count, 1)
        pieces.append(jnp.where(me == row_first // units, candidate, jnp.bfloat16(0.0)))
    contribution = jnp.concatenate(pieces, axis=1)
    usable = jnp.broadcast_to(
        (token_ids < special_first).astype(jnp.float32)[:, None], contribution.shape
    )
    return add_slab(LINE * PAIR * 2, contribution, usable, keys, prior_slab)


def solution(mesh):
    in_specs = (
        P("parts"),
        P("parts"),
        P(("parts", "wide"), None),
        P(None, ("wide", "narrow")),
        P(None, ("wide", "narrow")),
        P(("parts", "narrow"), "wide"),
    )
    out_specs = P(("parts", "narrow"), "wide")
    shards = fused_shards if mesh.shape["wide"] == LINE * PAIR else plain_shards
    return jax.shard_map(shards, mesh=mesh, in_specs=in_specs, out_specs=out_specs, check_vma=False)
```

```python
import functools

import jax
import jax.numpy as jnp
from jax import lax
from jax.experimental import pallas as pl
from jax.experimental.pallas import tpu as pltpu
from jax.sharding import PartitionSpec as P

special_first = 128000
LINE = 4
PAIR = 2
AHEAD = 4
MESH = pl.DeviceIdType.MESH


def make_keys(features, gate_weight, up_weight):
    gate_sum = jnp.dot(features, gate_weight, preferred_element_type=jnp.float32)
    up_sum = jnp.dot(features, up_weight, preferred_element_type=jnp.float32)
    return (jax.nn.silu(gate_sum) * up_sum).astype(jnp.bfloat16)


def plain_shards(token_ids, slab_offset, activations, gate_weight, up_weight, prior_slab):
    key_rows = make_keys(
        lax.all_gather(activations, "wide", axis=0, tiled=True), gate_weight, up_weight
    )
    columns = lax.all_gather(key_rows, "narrow", axis=1, tiled=True)
    column_count = columns.shape[1]
    row_count = prior_slab.shape[0]
    row_first = slab_offset[0] + lax.axis_index("narrow") * row_count
    holder = row_first // column_count
    inside = row_first % column_count
    candidate = lax.dynamic_slice_in_dim(columns, inside, row_count, 1)
    contribution = jnp.where(
        lax.axis_index("wide") == holder, candidate.astype(jnp.float32), jnp.float32(0.0)
    )
    selected = lax.psum(contribution.astype(jnp.bfloat16), "wide")
    usable = (token_ids < special_first).astype(jnp.bfloat16)[:, None]
    masked = selected * usable
    product = lax.dot_general(
        masked, columns, (((0,), (0,)), ((), ())), preferred_element_type=jnp.float32
    )
    return prior_slab + product


def keys_kernel(
    act, wg, wu, keys, gath, w_v, x_v, k_v,
    w_sem, x_sem, k_sem, up_send, up_recv, down_send, down_recv, side_send, side_recv,
    core_send, core_recv, cross_send, cross_recv,
):
    wide = lax.axis_index("wide")
    core = lax.axis_index("narrow")
    z, y = wide // PAIR, wide % PAIR
    rows = act.shape[0]
    piece = rows // 4
    tiles = w_v.shape[0]
    odd = lax.rem(z, 2)
    up = lax.rem(z + 1, LINE) * PAIR + y
    down = lax.rem(z + LINE - 1, LINE) * PAIR + y
    side = z * PAIR + 1 - y
    cross = (z + 1 - 2 * odd) * PAIR + y

    barrier = pltpu.get_barrier_semaphore()
    for w in (up, down, side):
        pl.semaphore_signal(
            barrier, inc=1, device_id={"wide": w, "narrow": core}, device_id_type=MESH
        )
    pl.semaphore_signal(
        barrier, inc=1, device_id={"wide": wide, "narrow": 1 - core}, device_id_type=MESH
    )

    own_load = pltpu.make_async_copy(act, x_v.at[0, pl.ds(0, rows), :], x_sem.at[0, 0])
    own_load.start()

    def w_copy(t, k):
        src = (wg, wu)[k]
        return pltpu.make_async_copy(
            src.at[:, pl.ds(pl.multiple_of(t * 128, 128), 128)],
            w_v.at[t, :, pl.ds(k * 128, 128)],
            w_sem.at[k, t],
        )

    pl.semaphore_wait(barrier, 4)

    def rows_of(b, c, s):
        return pl.ds(pl.multiple_of(b * rows + (c * 2 + s) * piece, 16), piece)

    order = (z, 1 + odd, lax.rem(z + 2, LINE), 3 - 3 * odd)

    def relay(b, s, own, target, ss, rs):
        if own:
            src = act.at[pl.ds(pl.multiple_of((core * 2 + s) * piece, 16), piece), :]
        else:
            src = gath.at[rows_of(b, core, s), :]
        return pltpu.make_async_remote_copy(
            src_ref=src, dst_ref=gath.at[rows_of(b, core, s), :], send_sem=ss, recv_sem=rs,
            device_id={"wide": target, "narrow": core}, device_id_type=MESH,
        )

    def send(kind, r, s):
        if kind == "up":
            b, t, ss, rs = (z - r) * PAIR + y, up, up_send, up_recv
        elif kind == "down":
            b, t, ss, rs = (z + r) * PAIR + y, down, down_send, down_recv
        elif kind == "side":
            b, t, ss, rs = order[r] * PAIR + y, side, side_send, side_recv
        else:
            b, t, ss, rs = 3 * odd * PAIR + 1 - y, cross, cross_send, cross_recv
        return relay(b, s, r == 0, t, ss.at[r, s], rs.at[r, s])

    def share(b, s):
        part = gath.at[rows_of(b, core, s), :]
        return pltpu.make_async_remote_copy(
            src_ref=part, dst_ref=part, send_sem=core_send.at[b, s], recv_sem=core_recv.at[b, s],
            device_id={"wide": wide, "narrow": 1 - core}, device_id_type=MESH,
        )

    def sends(kind, r):
        if kind == "up":
            return jnp.logical_and(z - r >= 0, z < LINE - 1)
        return jnp.logical_and(z + r < LINE, z > 0)

    def receives(kind, r):
        return z - 1 - r >= 0 if kind == "up" else z + 1 + r < LINE

    def last_kind(s):
        return ("side", "cross")[s]

    def push(r, s):
        if r == LINE - 1:
            send(last_kind(s), r, s).start()
            return
        for kind in ("up", "down"):
            @pl.when(sends(kind, r))
            def _():
                send(kind, r, s).start()
        send("side", r, s).start()

    def arrive(r, s):
        if r == LINE - 1:
            send(last_kind(s), r, s).wait_recv()
        else:
            for kind in ("up", "down"):
                @pl.when(receives(kind, r))
                def _():
                    send(kind, r, s).wait_recv()
            send("side", r, s).wait_recv()
            push(r + 1, s)
            for kind in ("up", "down"):
                @pl.when(receives(kind, r))
                def _():
                    block = z - 1 - r if kind == "up" else z + 1 + r
                    share(block * PAIR + y, s).start()
        share(order[r] * PAIR + 1 - y, s).start()

    def tile(t, slot, first, count):
        acc = jnp.dot(
            x_v[slot, first:first + count, :], w_v[t], preferred_element_type=jnp.float32
        )
        g, u = acc[:, :128], acc[:, 128:]
        k_v[first:first + count, pl.ds(pl.multiple_of(t * 128, 128), 128)] = (
            g / (1.0 + jnp.exp(-g)) * u
        ).astype(jnp.bfloat16)

    def fetch(blocks, s, slot):
        loads, spans = [], []
        for b in blocks:
            share(b, s).wait_recv()
            for c in range(2):
                k = s * 4 + len(spans)
                spans.append(rows_of(b, c, s))
                load = pltpu.make_async_copy(
                    gath.at[spans[-1], :],
                    x_v.at[slot, pl.ds(k * piece, piece), :],
                    x_sem.at[slot, k],
                )
                load.start()
                loads.append(load)
        return loads, spans

    def finish(copies):
        for copy in copies:
            copy.wait()

    def store(spans, first):
        copies = []
        for k, span in enumerate(spans, first // piece):
            copies.append(
                pltpu.make_async_copy(
                    k_v.at[pl.ds(k * piece, piece), :], keys.at[span, :], k_sem.at[k]
                )
            )
            copies[-1].start()
        return copies

    def multiply(slot, first, count, start, stop):
        @pl.loop(start, stop)
        def _(t):
            tile(t, slot, first, count)

    def pair(r):
        return order[r] * PAIR + 1 - y, order[r + 1] * PAIR + y

    for s in range(2):
        push(0, s)
    ahead = min(AHEAD, tiles)
    for t in range(ahead):
        w_copy(t, 0).start()
        w_copy(t, 1).start()
    own_load.wait()

    def first_tile(t):
        w_copy(t, 0).wait()
        w_copy(t, 1).wait()

        @pl.when(t + ahead < tiles)
        def _():
            w_copy(t + ahead, 0).start()
            w_copy(t + ahead, 1).start()

        tile(t, 0, 0, rows)

    pl.loop(0, tiles // 2)(first_tile)
    arrive(0, 0)
    pl.loop(tiles // 2, tiles - 1)(first_tile)
    loads, spans = fetch(pair(0), 0, 1)
    arrive(0, 1)
    pl.loop(tiles - 1, tiles)(first_tile)
    own_store = store([rows_of(z * PAIR + y, k // 2, k % 2) for k in range(4)], 0)
    more, rest = fetch(pair(0), 1, 1)
    finish(loads + more + own_store)
    early = (9 * tiles) // 13
    multiply(1, 0, 2 * rows, 0, early)
    arrive(1, 0)
    multiply(1, 0, 2 * rows, early, tiles - 1)
    loads, ahead_spans = fetch(pair(1), 0, 0)
    multiply(1, 0, 2 * rows, tiles - 1, tiles)
    stores = store(spans + rest, 0)
    done = [stores[:4], stores[4:]]
    spans = ahead_spans
    last = order[LINE - 1] * PAIR + 1 - y
    for r, s, at in ((1, 0, 8), (1, 1, 10), (2, 0, 10), (2, 1, 11)):
        slot, first = r - 1, s * rows
        finish(loads + done[s])
        at = (at * tiles) // 13
        multiply(slot, first, rows, 0, at)
        if r < LINE - 2 or s == 0:
            arrive(r + s, 1 - s)
            multiply(slot, first, rows, at, tiles)
            done[s] = store(spans, first)
            loads, spans = fetch(pair(r + s), 1 - s, r + s - 1)
        else:
            arrive(r + 1, 0)
            multiply(slot, first, rows, at, tiles)
            done[s] = store(spans, first)
            arrive(r + 1, 1)
            for t in range(2):
                share(last, t).wait_recv()
            load = pltpu.make_async_copy(
                gath.at[pl.ds(pl.multiple_of(last * rows, 16), rows), :],
                x_v.at[0, pl.ds(0, rows), :],
                x_sem.at[0, 0],
            )
            load.start()
            loads = [load]
    finish(loads + done[0])
    multiply(0, 0, rows, 0, tiles)
    finish(store([rows_of(last, k // 2, k % 2) for k in range(4)], 0) + done[1])
    for s in range(2):
        for r in range(LINE):
            share(order[r] * PAIR + 1 - y, s).wait_send()
            if r:
                share(order[r] * PAIR + y, s).wait_send()
            if r == LINE - 1:
                send(last_kind(s), r, s).wait_send()
            else:
                send("side", r, s).wait_send()
                for kind in ("up", "down"):
                    @pl.when(sends(kind, r))
                    def _():
                        send(kind, r, s).wait_send()


def make_key_rows(activations, gate_weight, up_weight):
    rows, features = activations.shape
    units = gate_weight.shape[1]
    tiles = units // 128
    tokens = rows * LINE * PAIR
    dma = pltpu.SemaphoreType.DMA
    return pl.pallas_call(
        keys_kernel,
        out_shape=(
            jax.ShapeDtypeStruct((tokens, units), jnp.bfloat16),
            jax.ShapeDtypeStruct((tokens, features), jnp.bfloat16),
        ),
        in_specs=[pl.BlockSpec(memory_space=pl.ANY)] * 3,
        out_specs=(pl.BlockSpec(memory_space=pl.ANY),) * 2,
        scratch_shapes=[
            pltpu.VMEM((tiles, features, 256), jnp.bfloat16),
            pltpu.VMEM((2, 2 * rows, features), jnp.bfloat16),
            pltpu.VMEM((2 * rows, units), jnp.bfloat16),
            dma((2, tiles)), dma((2, 8)), dma((8,)),
            dma((LINE, 2)), dma((LINE, 2)), dma((LINE, 2)), dma((LINE, 2)),
            dma((LINE, 2)), dma((LINE, 2)), dma((LINE * PAIR, 2)), dma((LINE * PAIR, 2)),
            dma((LINE, 2)), dma((LINE, 2)),
        ],
        compiler_params=pltpu.CompilerParams(
            collective_id=0, has_side_effects=True, vmem_limit_bytes=63 * 1024 * 1024
        ),
        name="gather_keys",
    )(activations, gate_weight, up_weight)[0]


def slab_kernel(
    group, contribution, usable, keys_hbm, prior_hbm, out, keys, prior, load_sem, land, sel,
    product, other,
    first_send, first_recv, second_send, second_recv, swap_send, swap_recv,
):
    loads = [
        pltpu.make_async_copy(keys_hbm, keys, load_sem.at[0]),
        pltpu.make_async_copy(prior_hbm, prior, load_sem.at[1]),
    ]
    for load in loads:
        load.start()
    wide = lax.axis_index("wide")
    core = lax.axis_index("narrow")
    me = wide * 2 + core
    span = land.shape[1]
    row_count = prior.shape[0]
    units = keys.shape[1]

    def rows_of(g):
        return pl.ds(pl.multiple_of(g * span, 16), span)

    def device(g):
        return {"wide": g // 2, "narrow": lax.rem(g, 2)}

    barrier = pltpu.get_barrier_semaphore()

    @pl.loop(1, group)
    def _(j):
        pl.semaphore_signal(
            barrier, inc=1, device_id=device(lax.rem(me + j, group)), device_id_type=MESH
        )

    pl.semaphore_wait(barrier, group - 1)

    def first(j):
        target = lax.rem(me + j, group)
        return pltpu.make_async_remote_copy(
            src_ref=contribution.at[rows_of(target), :], dst_ref=land.at[j - 1],
            send_sem=first_send.at[j - 1], recv_sem=first_recv.at[j - 1],
            device_id=device(target), device_id_type=MESH,
        )

    def second(j, owner):
        return pltpu.make_async_remote_copy(
            src_ref=sel.at[rows_of(owner), :], dst_ref=sel.at[rows_of(owner), :],
            send_sem=second_send.at[j - 1], recv_sem=second_recv.at[j - 1],
            device_id=device(lax.rem(me + j, group)), device_id_type=MESH,
        )

    @pl.loop(1, group)
    def _(j):
        first(j).start()

    @pl.loop(1, group)
    def _(j):
        first(j).wait_recv()

    total = contribution[rows_of(me), :].astype(jnp.float32)
    for j in range(1, group):
        total = total + land[j - 1].astype(jnp.float32)
    sel[rows_of(me), :] = (total * usable[rows_of(me), :]).astype(jnp.bfloat16)

    @pl.loop(1, group)
    def _(j):
        second(j, me).start()

    @pl.loop(1, group)
    def _(j):
        second(j, lax.rem(me + group - j, group)).wait_recv()

    for load in loads:
        load.wait()
    product[...] = lax.dot_general(
        sel[...], keys[...], (((0,), (0,)), ((), ())), preferred_element_type=jnp.float32
    ).reshape(2, row_count, units)

    swap = pltpu.make_async_remote_copy(
        src_ref=product.at[1 - core], dst_ref=other,
        send_sem=swap_send, recv_sem=swap_recv,
        device_id={"wide": wide, "narrow": 1 - core}, device_id_type=MESH,
    )
    swap.start()
    mine = pl.ds(pl.multiple_of(core * units, 128), units)
    theirs = pl.ds(pl.multiple_of((1 - core) * units, 128), units)
    out[:, mine] = prior[:, mine] + product[core]
    swap.wait_recv()
    out[:, theirs] = prior[:, theirs] + other[...]
    swap.wait_send()

    @pl.loop(1, group)
    def _(j):
        first(j).wait_send()
        second(j, me).wait_send()


def add_slab(group, contribution, usable, keys, prior):
    tokens, units = keys.shape
    row_count, slab_columns = prior.shape
    span = tokens // group
    dma = pltpu.SemaphoreType.DMA
    vmem = pl.BlockSpec(memory_space=pltpu.VMEM)
    return pl.pallas_call(
        functools.partial(slab_kernel, group),
        out_shape=jax.ShapeDtypeStruct(prior.shape, jnp.float32),
        in_specs=[vmem] * 2 + [pl.BlockSpec(memory_space=pl.ANY)] * 2,
        out_specs=vmem,
        scratch_shapes=[
            pltpu.VMEM(keys.shape, jnp.bfloat16),
            pltpu.VMEM(prior.shape, jnp.float32),
            dma((2,)),
            pltpu.VMEM((group - 1, span, 2 * row_count), jnp.bfloat16),
            pltpu.VMEM((tokens, 2 * row_count), jnp.bfloat16),
            pltpu.VMEM((2, row_count, units), jnp.float32),
            pltpu.VMEM((row_count, units), jnp.float32),
            dma((group - 1,)), dma((group - 1,)), dma((group - 1,)), dma((group - 1,)),
            dma, dma,
        ],
        compiler_params=pltpu.CompilerParams(
            collective_id=1, has_side_effects=True, vmem_limit_bytes=40 * 1024 * 1024
        ),
        name="slab_product",
    )(contribution, usable, keys, prior)


def fused_shards(token_ids, slab_offset, activations, gate_weight, up_weight, prior_slab):
    keys = make_key_rows(activations, gate_weight, up_weight)
    units = keys.shape[1]
    row_count = prior_slab.shape[0]
    me = lax.axis_index("wide") * 2 + lax.axis_index("narrow")
    pieces = []
    for k in range(2):
        row_first = slab_offset[0] + k * row_count
        candidate = lax.dynamic_slice_in_dim(keys, row_first % units, row_count, 1)
        pieces.append(jnp.where(me == row_first // units, candidate, jnp.bfloat16(0.0)))
    contribution = jnp.concatenate(pieces, axis=1)
    usable = jnp.broadcast_to(
        (token_ids < special_first).astype(jnp.float32)[:, None], contribution.shape
    )
    return add_slab(LINE * PAIR * 2, contribution, usable, keys, prior_slab)


def solution(mesh):
    in_specs = (
        P("parts"),
        P("parts"),
        P(("parts", "wide"), None),
        P(None, ("wide", "narrow")),
        P(None, ("wide", "narrow")),
        P(("parts", "narrow"), "wide"),
    )
    out_specs = P(("parts", "narrow"), "wide")
    shards = fused_shards if mesh.shape["wide"] == LINE * PAIR else plain_shards
    return jax.shard_map(shards, mesh=mesh, in_specs=in_specs, out_specs=out_specs, check_vma=False)
```

```python
import functools

import jax
import jax.numpy as jnp
from jax import lax
from jax.experimental import pallas as pl
from jax.experimental.pallas import tpu as pltpu
from jax.sharding import PartitionSpec as P

special_first = 128000
LINE = 4
PAIR = 2
AHEAD = 4
MESH = pl.DeviceIdType.MESH


def make_keys(features, gate_weight, up_weight):
    gate_sum = jnp.dot(features, gate_weight, preferred_element_type=jnp.float32)
    up_sum = jnp.dot(features, up_weight, preferred_element_type=jnp.float32)
    return (jax.nn.silu(gate_sum) * up_sum).astype(jnp.bfloat16)


def plain_shards(token_ids, slab_offset, activations, gate_weight, up_weight, prior_slab):
    key_rows = make_keys(
        lax.all_gather(activations, "wide", axis=0, tiled=True), gate_weight, up_weight
    )
    columns = lax.all_gather(key_rows, "narrow", axis=1, tiled=True)
    column_count = columns.shape[1]
    row_count = prior_slab.shape[0]
    row_first = slab_offset[0] + lax.axis_index("narrow") * row_count
    holder = row_first // column_count
    inside = row_first % column_count
    candidate = lax.dynamic_slice_in_dim(columns, inside, row_count, 1)
    contribution = jnp.where(
        lax.axis_index("wide") == holder, candidate.astype(jnp.float32), jnp.float32(0.0)
    )
    selected = lax.psum(contribution.astype(jnp.bfloat16), "wide")
    usable = (token_ids < special_first).astype(jnp.bfloat16)[:, None]
    masked = selected * usable
    product = lax.dot_general(
        masked, columns, (((0,), (0,)), ((), ())), preferred_element_type=jnp.float32
    )
    return prior_slab + product


def keys_kernel(
    act, wg, wu, keys, gath, w_v, x_v, k_v,
    w_sem, x_sem, k_sem, up_send, up_recv, down_send, down_recv, side_send, side_recv,
    core_send, core_recv, cross_send, cross_recv,
):
    wide = lax.axis_index("wide")
    core = lax.axis_index("narrow")
    z, y = wide // PAIR, wide % PAIR
    rows = act.shape[0]
    piece = rows // 4
    tiles = w_v.shape[0]
    odd = lax.rem(z, 2)
    up = lax.rem(z + 1, LINE) * PAIR + y
    down = lax.rem(z + LINE - 1, LINE) * PAIR + y
    side = z * PAIR + 1 - y
    cross = (z + 1 - 2 * odd) * PAIR + y

    barrier = pltpu.get_barrier_semaphore()
    for w in (up, down, side):
        pl.semaphore_signal(
            barrier, inc=1, device_id={"wide": w, "narrow": core}, device_id_type=MESH
        )
    pl.semaphore_signal(
        barrier, inc=1, device_id={"wide": wide, "narrow": 1 - core}, device_id_type=MESH
    )

    own_load = pltpu.make_async_copy(act, x_v.at[0, pl.ds(0, rows), :], x_sem.at[0, 0])
    own_load.start()

    def w_copy(t, k):
        src = (wg, wu)[k]
        return pltpu.make_async_copy(
            src.at[:, pl.ds(pl.multiple_of(t * 128, 128), 128)],
            w_v.at[t, :, pl.ds(k * 128, 128)],
            w_sem.at[k, t],
        )

    pl.semaphore_wait(barrier, 4)

    def rows_of(b, c, s):
        return pl.ds(pl.multiple_of(b * rows + (c * 2 + s) * piece, 16), piece)

    order = (z, 1 + odd, lax.rem(z + 2, LINE), 3 - 3 * odd)

    def relay(b, s, own, target, ss, rs):
        if own:
            src = act.at[pl.ds(pl.multiple_of((core * 2 + s) * piece, 16), piece), :]
        else:
            src = gath.at[rows_of(b, core, s), :]
        return pltpu.make_async_remote_copy(
            src_ref=src, dst_ref=gath.at[rows_of(b, core, s), :], send_sem=ss, recv_sem=rs,
            device_id={"wide": target, "narrow": core}, device_id_type=MESH,
        )

    def send(kind, r, s):
        if kind == "up":
            b, t, ss, rs = (z - r) * PAIR + y, up, up_send, up_recv
        elif kind == "down":
            b, t, ss, rs = (z + r) * PAIR + y, down, down_send, down_recv
        elif kind == "side":
            b, t, ss, rs = order[r] * PAIR + y, side, side_send, side_recv
        else:
            b, t, ss, rs = 3 * odd * PAIR + 1 - y, cross, cross_send, cross_recv
        return relay(b, s, r == 0, t, ss.at[r, s], rs.at[r, s])

    def share(b, s):
        part = gath.at[rows_of(b, core, s), :]
        return pltpu.make_async_remote_copy(
            src_ref=part, dst_ref=part, send_sem=core_send.at[b, s], recv_sem=core_recv.at[b, s],
            device_id={"wide": wide, "narrow": 1 - core}, device_id_type=MESH,
        )

    def sends(kind, r):
        if kind == "up":
            return jnp.logical_and(z - r >= 0, z < LINE - 1)
        return jnp.logical_and(z + r < LINE, z > 0)

    def receives(kind, r):
        return z - 1 - r >= 0 if kind == "up" else z + 1 + r < LINE

    def last_kind(s):
        return ("side", "cross")[s]

    def push(r, s):
        if r == LINE - 1:
            send(last_kind(s), r, s).start()
            return
        for kind in ("up", "down"):
            @pl.when(sends(kind, r))
            def _():
                send(kind, r, s).start()
        send("side", r, s).start()

    def arrive(r, s):
        if r == LINE - 1:
            send(last_kind(s), r, s).wait_recv()
        else:
            for kind in ("up", "down"):
                @pl.when(receives(kind, r))
                def _():
                    send(kind, r, s).wait_recv()
            send("side", r, s).wait_recv()
            push(r + 1, s)
            for kind in ("up", "down"):
                @pl.when(receives(kind, r))
                def _():
                    block = z - 1 - r if kind == "up" else z + 1 + r
                    share(block * PAIR + y, s).start()
        share(order[r] * PAIR + 1 - y, s).start()

    def tile(t, slot, first, count):
        acc = jnp.dot(
            x_v[slot, first:first + count, :], w_v[t], preferred_element_type=jnp.float32
        )
        g, u = acc[:, :128], acc[:, 128:]
        k_v[first:first + count, pl.ds(pl.multiple_of(t * 128, 128), 128)] = (
            g / (1.0 + jnp.exp(-g)) * u
        ).astype(jnp.bfloat16)

    def fetch(blocks, s, slot):
        loads, spans = [], []
        for b in blocks:
            share(b, s).wait_recv()
            for c in range(2):
                k = s * 4 + len(spans)
                spans.append(rows_of(b, c, s))
                load = pltpu.make_async_copy(
                    gath.at[spans[-1], :],
                    x_v.at[slot, pl.ds(k * piece, piece), :],
                    x_sem.at[slot, k],
                )
                load.start()
                loads.append(load)
        return loads, spans

    def finish(copies):
        for copy in copies:
            copy.wait()

    def store(spans, first):
        copies = []
        for k, span in enumerate(spans, first // piece):
            copies.append(
                pltpu.make_async_copy(
                    k_v.at[pl.ds(k * piece, piece), :], keys.at[span, :], k_sem.at[k]
                )
            )
            copies[-1].start()
        return copies

    def multiply(slot, first, count, start, stop):
        @pl.loop(start, stop)
        def _(t):
            tile(t, slot, first, count)

    def pair(r):
        return order[r] * PAIR + 1 - y, order[r + 1] * PAIR + y

    for s in range(2):
        push(0, s)
    ahead = min(AHEAD, tiles)
    for t in range(ahead):
        w_copy(t, 0).start()
        w_copy(t, 1).start()
    own_load.wait()

    def first_tile(t):
        w_copy(t, 0).wait()
        w_copy(t, 1).wait()

        @pl.when(t + ahead < tiles)
        def _():
            w_copy(t + ahead, 0).start()
            w_copy(t + ahead, 1).start()

        tile(t, 0, 0, rows)

    pl.loop(0, tiles // 2)(first_tile)
    arrive(0, 0)
    pl.loop(tiles // 2, tiles - 1)(first_tile)
    loads, spans = fetch(pair(0), 0, 1)
    arrive(0, 1)
    pl.loop(tiles - 1, tiles)(first_tile)
    own_store = store([rows_of(z * PAIR + y, k // 2, k % 2) for k in range(4)], 0)
    more, rest = fetch(pair(0), 1, 1)
    finish(loads + more + own_store)
    early = (9 * tiles) // 13
    multiply(1, 0, 2 * rows, 0, early)
    arrive(1, 0)
    multiply(1, 0, 2 * rows, early, tiles - 1)
    loads, ahead_spans = fetch(pair(1), 0, 0)
    multiply(1, 0, 2 * rows, tiles - 1, tiles)
    stores = store(spans + rest, 0)
    done = [stores[:4], stores[4:]]
    spans = ahead_spans
    last = order[LINE - 1] * PAIR + 1 - y
    for r, s, at in ((1, 0, 8), (1, 1, 10), (2, 0, 10), (2, 1, 11)):
        slot, first = r - 1, s * rows
        finish(loads + done[s])
        at = (at * tiles) // 13
        multiply(slot, first, rows, 0, at)
        if r < LINE - 2 or s == 0:
            arrive(r + s, 1 - s)
            multiply(slot, first, rows, at, tiles)
            done[s] = store(spans, first)
            loads, spans = fetch(pair(r + s), 1 - s, r + s - 1)
        else:
            arrive(r + 1, 0)
            multiply(slot, first, rows, at, tiles)
            done[s] = store(spans, first)
            arrive(r + 1, 1)
            for t in range(2):
                share(last, t).wait_recv()
            load = pltpu.make_async_copy(
                gath.at[pl.ds(pl.multiple_of(last * rows, 16), rows), :],
                x_v.at[0, pl.ds(0, rows), :],
                x_sem.at[0, 0],
            )
            load.start()
            loads = [load]
    finish(loads + done[0])
    multiply(0, 0, rows, 0, tiles)
    finish(store([rows_of(last, k // 2, k % 2) for k in range(4)], 0) + done[1])
    for s in range(2):
        for r in range(LINE):
            share(order[r] * PAIR + 1 - y, s).wait_send()
            if r:
                share(order[r] * PAIR + y, s).wait_send()
            if r == LINE - 1:
                send(last_kind(s), r, s).wait_send()
            else:
                send("side", r, s).wait_send()
                for kind in ("up", "down"):
                    @pl.when(sends(kind, r))
                    def _():
                        send(kind, r, s).wait_send()


def make_key_rows(activations, gate_weight, up_weight):
    rows, features = activations.shape
    units = gate_weight.shape[1]
    tiles = units // 128
    tokens = rows * LINE * PAIR
    dma = pltpu.SemaphoreType.DMA
    return pl.pallas_call(
        keys_kernel,
        out_shape=(
            jax.ShapeDtypeStruct((tokens, units), jnp.bfloat16),
            jax.ShapeDtypeStruct((tokens, features), jnp.bfloat16),
        ),
        in_specs=[pl.BlockSpec(memory_space=pl.ANY)] * 3,
        out_specs=(pl.BlockSpec(memory_space=pl.ANY),) * 2,
        scratch_shapes=[
            pltpu.VMEM((tiles, features, 256), jnp.bfloat16),
            pltpu.VMEM((2, 2 * rows, features), jnp.bfloat16),
            pltpu.VMEM((2 * rows, units), jnp.bfloat16),
            dma((2, tiles)), dma((2, 8)), dma((8,)),
            dma((LINE, 2)), dma((LINE, 2)), dma((LINE, 2)), dma((LINE, 2)),
            dma((LINE, 2)), dma((LINE, 2)), dma((LINE * PAIR, 2)), dma((LINE * PAIR, 2)),
            dma((LINE, 2)), dma((LINE, 2)),
        ],
        compiler_params=pltpu.CompilerParams(
            collective_id=0, has_side_effects=True, vmem_limit_bytes=63 * 1024 * 1024
        ),
        name="gather_keys",
    )(activations, gate_weight, up_weight)[0]


def slab_kernel(
    group, contribution, usable, keys_hbm, prior_hbm, out, keys, prior, load_sem, land, sel,
    product, other, mix, twin_half, twin_send, twin_recv,
    first_send, first_recv, second_send, second_recv, swap_send, swap_recv,
):
    loads = [
        pltpu.make_async_copy(keys_hbm, keys, load_sem.at[0]),
        pltpu.make_async_copy(prior_hbm, prior, load_sem.at[1]),
    ]
    for load in loads:
        load.start()
    wide = lax.axis_index("wide")
    core = lax.axis_index("narrow")
    span = land.shape[1]
    half = mix.shape[0]
    row_count = prior.shape[0]
    units = keys.shape[1]
    twin = {"wide": wide, "narrow": 1 - core}

    def peer(j):
        return {"wide": lax.rem(wide + j, group), "narrow": core}

    def half_of(c):
        return pl.ds(pl.multiple_of(c * half, 16), half)

    def rows_of(w):
        return pl.ds(pl.multiple_of(w * span, 16), span)

    def slice_of(w):
        return pl.ds(pl.multiple_of(core * half + w * span, 16), span)

    barrier = pltpu.get_barrier_semaphore()

    @pl.loop(1, group)
    def _(j):
        pl.semaphore_signal(barrier, inc=1, device_id=peer(j), device_id_type=MESH)

    pl.semaphore_signal(barrier, inc=1, device_id=twin, device_id_type=MESH)
    pl.semaphore_wait(barrier, group)

    def first(j):
        return pltpu.make_async_remote_copy(
            src_ref=mix.at[rows_of(lax.rem(wide + j, group)), :], dst_ref=land.at[j - 1],
            send_sem=first_send.at[j - 1], recv_sem=first_recv.at[j - 1],
            device_id=peer(j), device_id_type=MESH,
        )

    def second(j, owner):
        return pltpu.make_async_remote_copy(
            src_ref=sel.at[slice_of(owner), :], dst_ref=sel.at[slice_of(owner), :],
            send_sem=second_send.at[j - 1], recv_sem=second_recv.at[j - 1],
            device_id=peer(j), device_id_type=MESH,
        )

    merge = pltpu.make_async_remote_copy(
        src_ref=contribution.at[half_of(1 - core), :], dst_ref=twin_half,
        send_sem=twin_send.at[0], recv_sem=twin_recv.at[0],
        device_id=twin, device_id_type=MESH,
    )
    merge.start()
    merge.wait_recv()
    mix[...] = contribution[half_of(core), :] + twin_half[...]

    @pl.loop(1, group)
    def _(j):
        first(j).start()

    @pl.loop(1, group)
    def _(j):
        first(j).wait_recv()

    total = mix[rows_of(wide), :].astype(jnp.float32)
    for j in range(1, group):
        total = total + land[j - 1].astype(jnp.float32)
    sel[slice_of(wide), :] = (total * usable[slice_of(wide), :]).astype(jnp.bfloat16)

    @pl.loop(1, group)
    def _(j):
        second(j, wide).start()

    @pl.loop(1, group)
    def _(j):
        second(j, lax.rem(wide + group - j, group)).wait_recv()

    spread = pltpu.make_async_remote_copy(
        src_ref=sel.at[half_of(core), :], dst_ref=sel.at[half_of(core), :],
        send_sem=twin_send.at[1], recv_sem=twin_recv.at[1],
        device_id=twin, device_id_type=MESH,
    )
    spread.start()
    spread.wait_recv()
    for load in loads:
        load.wait()
    product[...] = lax.dot_general(
        sel[...], keys[...], (((0,), (0,)), ((), ())), preferred_element_type=jnp.float32
    ).reshape(2, row_count, units)

    swap = pltpu.make_async_remote_copy(
        src_ref=product.at[1 - core], dst_ref=other,
        send_sem=swap_send, recv_sem=swap_recv,
        device_id={"wide": wide, "narrow": 1 - core}, device_id_type=MESH,
    )
    swap.start()
    mine = pl.ds(pl.multiple_of(core * units, 128), units)
    theirs = pl.ds(pl.multiple_of((1 - core) * units, 128), units)
    out[:, mine] = prior[:, mine] + product[core]
    swap.wait_recv()
    out[:, theirs] = prior[:, theirs] + other[...]
    swap.wait_send()

    @pl.loop(1, group)
    def _(j):
        first(j).wait_send()
        second(j, wide).wait_send()

    merge.wait_send()
    spread.wait_send()


def add_slab(group, contribution, usable, keys, prior):
    tokens, units = keys.shape
    row_count, slab_columns = prior.shape
    span = tokens // (2 * group)
    dma = pltpu.SemaphoreType.DMA
    vmem = pl.BlockSpec(memory_space=pltpu.VMEM)
    return pl.pallas_call(
        functools.partial(slab_kernel, group),
        out_shape=jax.ShapeDtypeStruct(prior.shape, jnp.float32),
        in_specs=[vmem] * 2 + [pl.BlockSpec(memory_space=pl.ANY)] * 2,
        out_specs=vmem,
        scratch_shapes=[
            pltpu.VMEM(keys.shape, jnp.bfloat16),
            pltpu.VMEM(prior.shape, jnp.float32),
            dma((2,)),
            pltpu.VMEM((group - 1, span, 2 * row_count), jnp.bfloat16),
            pltpu.VMEM((tokens, 2 * row_count), jnp.bfloat16),
            pltpu.VMEM((2, row_count, units), jnp.float32),
            pltpu.VMEM((row_count, units), jnp.float32),
            pltpu.VMEM((tokens // 2, 2 * row_count), jnp.bfloat16),
            pltpu.VMEM((tokens // 2, 2 * row_count), jnp.bfloat16),
            dma((2,)), dma((2,)),
            dma((group - 1,)), dma((group - 1,)), dma((group - 1,)), dma((group - 1,)),
            dma, dma,
        ],
        compiler_params=pltpu.CompilerParams(
            collective_id=1, has_side_effects=True, vmem_limit_bytes=40 * 1024 * 1024
        ),
        name="slab_product",
    )(contribution, usable, keys, prior)


def fused_shards(token_ids, slab_offset, activations, gate_weight, up_weight, prior_slab):
    keys = make_key_rows(activations, gate_weight, up_weight)
    units = keys.shape[1]
    row_count = prior_slab.shape[0]
    me = lax.axis_index("wide") * 2 + lax.axis_index("narrow")
    pieces = []
    for k in range(2):
        row_first = slab_offset[0] + k * row_count
        candidate = lax.dynamic_slice_in_dim(keys, row_first % units, row_count, 1)
        pieces.append(jnp.where(me == row_first // units, candidate, jnp.bfloat16(0.0)))
    contribution = jnp.concatenate(pieces, axis=1)
    usable = jnp.broadcast_to(
        (token_ids < special_first).astype(jnp.float32)[:, None], contribution.shape
    )
    return add_slab(LINE * PAIR, contribution, usable, keys, prior_slab)


def solution(mesh):
    in_specs = (
        P("parts"),
        P("parts"),
        P(("parts", "wide"), None),
        P(None, ("wide", "narrow")),
        P(None, ("wide", "narrow")),
        P(("parts", "narrow"), "wide"),
    )
    out_specs = P(("parts", "narrow"), "wide")
    shards = fused_shards if mesh.shape["wide"] == LINE * PAIR else plain_shards
    return jax.shard_map(shards, mesh=mesh, in_specs=in_specs, out_specs=out_specs, check_vma=False)
```
